32 devices in a mesh: grp: 2 (over x), tok: 8 (over z, y), ep: 2 (over core).
Axes of the slice: x: 2, y: 2, z: 4, core: 2. Of those that a mesh axis runs over, the one named last changes fastest.
Arguments:
- tokens: bfloat16 [2, 2048, 768], P('ep', ('grp', 'tok')), parts along dimension 1, may hold values from -6 to 6
- norm_gain: float32 [768], replicated, may hold values from 0.5 to 1.5
- query_weight: bfloat16 [768, 768], replicated, may hold values from -0.21875 to 0.21875
- w_key: bfloat16 [768, 768], replicated, may hold values from -0.21875 to 0.21875
- w_value: bfloat16 [768, 768], replicated, may hold values from -0.21875 to 0.21875
- w_out: bfloat16 [768, 768], replicated, may hold values from -0.21875 to 0.21875
- head_scale: float32 [12], replicated, may hold values from 0.5 to 64
- matching: int32 [2, 64], P('ep', ('grp', 'tok')), parts along dimension 1, may hold values from 0 to 3, as said below
- valid: int32 [2, 64], P('ep', ('grp', 'tok')), parts along dimension 1, may hold values from 1 to 32, as said below
- stops: int32 [2, 16, 4], P('ep', ('grp', 'tok')), parts along dimension 1, may hold values from 0 to 7, as said below
Outputs:
- refined: bfloat16 [2, 2048, 768], P('ep', ('grp', 'tok')), parts along dimension 1
The draws below stay inside these ranges and needn't reach their ends.
There are 2 independent parts, one for each index of `grp`. The reference program is written for one: setup_inputs(seed, part) draws one part's arguments, and reference() takes and returns one part's arrays. A program takes and returns all parts, laid end to end along the dimension named above; an argument that names none is the same for every part. Nothing has to cross between parts.
Inputs may be any that keep to these rules, and one draw needn't show every extreme that they name: `matching`: each aligned group of 4 entries is a permutation of 0 to 3. `valid`: in every block of 4 tiles one tile is full. `stops`: the 4 entries of block t are distinct blocks within 3 of t, and one of them is t - 3 or t + 3.
All inputs are finite; a program needn't handle non-finite values.
Results may differ from the reference program's by a relative error of at most 0.004.
The reference program's roundings to bfloat16 on the way count: a program that leaves them out, or rounds other values in their place, can miss the bound.
Values may be sent and summed in bfloat16 or wider, within the bound.
A program may use at most 64 MiB of HBM per device.

```python
import math
import jax
import jax.numpy as jnp
from jax import lax

D = 768
H = 12
HD = 64
TOK_DEV = 128
TILE = 32
BAND = 3
STOPS = 4
ROW_PATCHES = 1024
TPD = 4
NBLK = 8
TOKENS = 1024
TILES = 32


def draw_head_scale(key, part):
    base = jnp.exp(jax.random.uniform(key, (H,), jnp.float32, math.log(0.5), math.log(2.0)))
    return base.astype(jnp.float32)


def draw_matching(key, part):
    subkeys = jax.random.split(jax.random.fold_in(key, 11), 2 * NBLK)

    def shuffle(subkey):
        return jax.random.permutation(subkey, TPD)
    orders = jax.vmap(shuffle)(subkeys)
    return orders.reshape(2, TILES).astype(jnp.int32)


def draw_valid(key, part):
    counts = jax.random.randint(jax.random.fold_in(key, 21), (2, NBLK, TPD), 1, TILE + 1)
    full_at = jax.random.randint(jax.random.fold_in(key, 22), (2, NBLK, 1), 0, TPD)
    slots = jnp.arange(TPD, dtype=jnp.int32)[None, None, :]
    counts = jnp.where(slots == full_at, TILE, counts)
    return counts.reshape(2, TILES).astype(jnp.int32)


def draw_stops(key, part):
    width = 2 * BAND + 1
    subkeys = jax.random.split(jax.random.fold_in(key, 31), 2 * NBLK)

    def shuffle(subkey):
        return jax.random.permutation(subkey, width)
    ranks = jax.vmap(shuffle)(subkeys).reshape(2, NBLK, width).astype(jnp.int32)
    blocks = jnp.arange(NBLK, dtype=jnp.int32)[None, :, None]
    offsets = jnp.arange(width, dtype=jnp.int32)[None, None, :] - BAND
    target = blocks + offsets
    inside = (target >= 0) & (target < NBLK)
    slots = jnp.arange(width, dtype=jnp.int32)[None, None, :]
    ranks = jnp.where(inside, ranks, -1 - slots)
    upward = jax.random.randint(jax.random.fold_in(key, 32), (2, NBLK, 1), 0, 2) == 1
    upper_fits = blocks + BAND < NBLK
    lower_fits = blocks - BAND >= 0
    take_upper = upper_fits & (upward | jnp.logical_not(lower_fits))
    forced = jnp.where(take_upper, width - 1, 0)
    ranks = jnp.where(slots == forced, 100, ranks)
    chosen = lax.top_k(ranks, STOPS)[1]
    return jnp.take_along_axis(target, chosen, axis=-1).astype(jnp.int32)


def steps_of(key, extent, cuts, smallest, largest):
    def one(axis_at, parts):
        steps = jax.random.uniform(jax.random.fold_in(jax.random.fold_in(key, 6), axis_at), (parts,), jnp.float32, smallest / len(cuts), largest / len(cuts))
        return jnp.repeat(jnp.exp(steps), extent[axis_at] // parts).reshape((-1,) + (1,) * (len(extent) - axis_at - 1))

    gain = one(*cuts[0])
    for cut in cuts[1:]:
        gain = gain * one(*cut)
    return gain


def normal_values(rng, shape, scale, bound, pieces=(), held_as=jnp.bfloat16):
    factor_of = steps_of(rng, shape, pieces, -0.22, 0.18) if pieces else 1.0
    drawn = jax.random.normal(rng, shape, jnp.float32) * scale * factor_of
    return jnp.minimum(jnp.maximum(drawn, -bound), bound).astype(held_as)


def setup_inputs(seed: int = 0, part: int = 0) -> dict:
    streams_of = jax.random.split(jax.random.key(seed), 11)
    own_keys = jax.random.split(jax.random.fold_in(streams_of[10], part), 11)
    tokens = normal_values(own_keys[0], (2, TOKENS, D), 1.0, 6.0, ((0, 2), (1, 8)))
    norm_gain = jnp.clip(1.0 + 0.1 * jax.random.normal(streams_of[1], (D,), jnp.float32), 0.5, 1.5)
    query_weight = normal_values(streams_of[2], (D, D), D ** -0.5, 0.21875)
    w_key = normal_values(streams_of[3], (D, D), D ** -0.5, 0.21875)
    w_value = normal_values(streams_of[4], (D, D), D ** -0.5, 0.21875)
    w_out = normal_values(streams_of[5], (D, D), D ** -0.5, 0.21875)
    head_scale = draw_head_scale(jax.random.fold_in(streams_of[10], 71), part)
    matching = draw_matching(jax.random.fold_in(jax.random.fold_in(streams_of[10], part), 71), part)
    valid = draw_valid(jax.random.fold_in(jax.random.fold_in(streams_of[10], part), 71), part)
    stops = draw_stops(jax.random.fold_in(jax.random.fold_in(streams_of[10], part), 71), part)
    return {"tokens": tokens, "norm_gain": norm_gain, "query_weight": query_weight, "w_key": w_key, "w_value": w_value, "w_out": w_out, "head_scale": head_scale, "matching": matching, "valid": valid, "stops": stops}


def layer_norm(floated, norm_gain):
    center = lax.optimization_barrier(jnp.mean(floated, axis=-1, keepdims=True))
    spread = lax.optimization_barrier(jnp.mean((floated - center) ** 2, axis=-1, keepdims=True))
    return (floated - center) * lax.rsqrt(spread + 1e-05) * norm_gain

def turn_pairs(part, angle):
    quarter = part.shape[-1] // 2
    first = part[..., :quarter]
    second = part[..., quarter:]
    cosine = jnp.cos(angle)[:, None, :]
    sine = jnp.sin(angle)[:, None, :]
    return jnp.concatenate([first * cosine - second * sine, second * cosine + first * sine], axis=-1)

def rotate(values, patch_coordinates, heads):
    count_rows, width = values.shape
    head_dim = width // heads
    half = head_dim // 2
    quarter = head_dim // 4
    split = values.reshape(count_rows, heads, head_dim)
    row_coordinate = (patch_coordinates // ROW_PATCHES).astype(jnp.float32)
    column_coordinate = (patch_coordinates % ROW_PATCHES).astype(jnp.float32)
    freqs = 100.0 ** (-jnp.arange(quarter, dtype=jnp.float32) / quarter)
    turned = jnp.concatenate([turn_pairs(split[..., :half], row_coordinate[:, None] * freqs[None, :]), turn_pairs(split[..., half:], column_coordinate[:, None] * freqs[None, :])], axis=-1)
    return turned.reshape(count_rows, width)

def reference(tokens, norm_gain, query_weight, w_key, w_value, w_out, head_scale, matching, valid, stops):
    floated = tokens.astype(jnp.float32)
    normed = layer_norm(floated, norm_gain).astype(jnp.bfloat16)
    patch_coordinates = jnp.arange(TOKENS, dtype=jnp.int32)
    scales = head_scale / math.sqrt(HD)
    results = []
    for epoch in range(2):
        source = 1 - epoch
        tile_ids = jnp.arange(TILES, dtype=jnp.int32) // TPD * TPD + matching[epoch]
        key_rows = normed[source].reshape(TILES, TILE, D)[tile_ids].reshape(TOKENS, D)
        counts = valid[source][tile_ids]
        live = (jnp.arange(TILE, dtype=jnp.int32)[None, :] < counts[:, None]).reshape(TOKENS)
        queries = rotate(jnp.dot(normed[epoch], query_weight, preferred_element_type=jnp.float32), patch_coordinates, H).astype(jnp.bfloat16)
        key_proj = rotate(jnp.dot(key_rows, w_key, preferred_element_type=jnp.float32), patch_coordinates, H).astype(jnp.bfloat16)
        value_proj = jnp.dot(key_rows, w_value, preferred_element_type=jnp.float32).astype(jnp.bfloat16)
        key_blocks = key_proj.reshape(NBLK, TOK_DEV, H, HD)
        value_blocks = value_proj.reshape(NBLK, TOK_DEV, H, HD)
        live_blocks = live.reshape(NBLK, TOK_DEV)
        query_blocks = queries.reshape(NBLK, TOK_DEV, H, HD)
        epoch_stops = stops[epoch]

        def one_block(block):
            chosen = epoch_stops[block]
            key_selection = key_blocks[chosen].reshape(STOPS * TOK_DEV, H, HD).astype(jnp.float32)
            value_sel = value_blocks[chosen].reshape(STOPS * TOK_DEV, H, HD).astype(jnp.float32)
            live_sel = live_blocks[chosen].reshape(STOPS * TOK_DEV)
            query_selection = query_blocks[block].astype(jnp.float32)
            scores = jnp.einsum('qhd,khd->hqk', query_selection, key_selection) * scales[:, None, None]
            scores = jnp.where(live_sel[None, None, :], scores, jnp.float32(-1e+30))
            best = lax.optimization_barrier(jnp.max(scores, axis=2, keepdims=True))
            weights = jnp.exp(scores - best)
            total = lax.optimization_barrier(jnp.sum(weights, axis=2))
            summed = jnp.einsum('hqk,khd->qhd', weights.astype(jnp.bfloat16).astype(jnp.float32), value_sel)
            return (summed / jnp.transpose(total)[:, :, None]).reshape(TOK_DEV, D).astype(jnp.bfloat16)
        attended = lax.map(one_block, jnp.arange(NBLK, dtype=jnp.int32)).reshape(TOKENS, D)
        mixed = floated[epoch] + jnp.dot(attended, w_out, preferred_element_type=jnp.float32)
        results.append(mixed.astype(jnp.bfloat16))
    return jnp.stack(results)
```

```python
import math

import jax
import jax.numpy as jnp
import numpy as np
from jax import lax
from jax.experimental import pallas as pl
from jax.experimental.pallas import tpu as pltpu
from jax.sharding import PartitionSpec as P

BAND = 3
ROW_PATCHES = 1024
LANES = 128
META = 16
MESH = pl.DeviceIdType.MESH
LOG2E = 1.4426950408889634


def rotary_table(blocks, rows, head_dim):
    quarter = head_dim // 4
    spots = np.arange(-BAND * rows, (blocks + BAND) * rows, dtype=np.int32)
    freqs = np.float32(100.0) ** (-np.arange(quarter, dtype=np.float32) / np.float32(quarter))
    parts = []
    for coordinate in (spots // ROW_PATCHES, spots % ROW_PATCHES):
        angle = coordinate.astype(np.float32)[:, None] * freqs[None, :].astype(np.float32)
        parts.append((np.cos(angle), np.sin(angle)))
    cosine = np.concatenate([half for c, _ in parts for half in (c, c)], axis=1)
    sine = np.concatenate([half for _, s in parts for half in (-s, s)], axis=1)
    copies = LANES // head_dim
    table = np.concatenate([cosine] * copies + [sine] * copies, axis=1)
    return table.reshape(blocks + 2 * BAND, rows, 2 * LANES).astype(np.float32)


def make_kernel(blocks, rows, width, heads, tiles):
    head_dim = width // heads
    quarter = head_dim // 4
    tile_rows = rows // tiles
    chunks = width // LANES
    per_chunk = LANES // head_dim
    slots = 2 * BAND + 1

    def turned(values, cosine, sine):
        lane = lax.broadcasted_iota(jnp.int32, values.shape, 1)
        ahead = pltpu.roll(values, LANES - quarter, 1)
        behind = pltpu.roll(values, quarter, 1)
        other = jnp.where(lane % (2 * quarter) < quarter, ahead, behind)
        return values * cosine + other * sine

    def kernel(
        tok_ref, gain_ref, scale_ref, match_ref, valid_ref, stops_ref,
        wq_hbm, wk_hbm, wv_hbm, wo_hbm, table_hbm,
        out_ref,
        wq, wk, wv, wo, table, mine, buf, match_out, match_in,
        queries, keys, values, masks, attended,
        local_sem, send_sem, recv_sem, match_sem,
    ):
        t = lax.axis_index("tok")
        ep = lax.axis_index("ep")
        other_ep = 1 - ep
        s = 1 - 2 * (t % 2)

        def there(k):
            spot = t + s * k
            return (spot >= 0) & (spot < blocks)

        def count(k):
            return there(k).astype(jnp.int32)

        loads = [
            pltpu.make_async_copy(table_hbm.at[pl.ds(t, slots)], table, local_sem.at[0]),
            pltpu.make_async_copy(wq_hbm, wq, local_sem.at[1]),
            pltpu.make_async_copy(wk_hbm, wk, local_sem.at[2]),
            pltpu.make_async_copy(wv_hbm, wv, local_sem.at[3]),
            pltpu.make_async_copy(wo_hbm, wo, local_sem.at[4]),
        ]

        barrier = pltpu.get_barrier_semaphore()

        def greet(tok, e):
            pl.semaphore_signal(
                barrier, inc=1, device_id={"tok": tok, "ep": e}, device_id_type=MESH
            )

        greet(t, other_ep)
        greet(t + s, ep)
        greet(t + s, other_ep)
        for k in (2, -2):
            @pl.when(there(k))
            def _():
                greet(t + s * k, ep)
                greet(t + s * k, other_ep)

        for load in loads:
            load.start()

        floated = tok_ref[0].astype(jnp.float32)
        center = jnp.mean(floated, axis=-1, keepdims=True)
        apart = floated - center
        spread = jnp.mean(apart * apart, axis=-1, keepdims=True)
        mine[:rows, :] = (apart * lax.rsqrt(spread + 1e-05) * gain_ref[...]).astype(jnp.bfloat16)

        row = lax.broadcasted_iota(jnp.int32, (8, LANES), 0)
        matched = jnp.zeros((8, LANES), jnp.float32)
        lane = lax.broadcasted_iota(jnp.int32, (8, rows), 1)
        live = jnp.zeros((8, rows), jnp.int32)
        for j in range(tiles):
            matched = jnp.where(row == j, match_ref[0, j].astype(jnp.float32), matched)
            live = jnp.where(lane // tile_rows == j, valid_ref[0, j], live)
        match_out[...] = matched
        hidden = jnp.where(lane % tile_rows < live, jnp.float32(0), jnp.float32(-1e30))

        pl.semaphore_wait(barrier, 3 + 2 * count(2) + 2 * count(-2))

        swap = pltpu.make_async_remote_copy(
            match_out, match_in, match_sem.at[0], match_sem.at[1],
            device_id={"tok": t, "ep": other_ep}, device_id_type=MESH,
        )
        swap.start()

        def transfer(src, number, slot, tok, e):
            return pltpu.make_async_remote_copy(
                src, buf.at[slot], send_sem.at[number], recv_sem.at[slot],
                device_id={"tok": tok, "ep": e}, device_id_type=MESH,
            )

        mid = BAND
        direct = [
            (2, transfer(mine, 0, mid - 2 * s, t + 2 * s, other_ep)),
            (-2, transfer(mine, 1, mid + 2 * s, t - 2 * s, other_ep)),
            (1, transfer(mine, 2, mid - s, t + s, other_ep)),
            (0, transfer(mine, 3, mid, t, other_ep)),
        ]
        relay_far = transfer(buf.at[mid + s], 4, mid + 3 * s, t - 2 * s, ep)
        relay_side = transfer(buf.at[mid + 2 * s], 5, mid + s, t + s, ep)
        relay_last = transfer(buf.at[mid - s], 6, mid - 3 * s, t + 2 * s, ep)
        last_there = there(2) & there(-1)

        def arrived(k):
            transfer(mine, 0, mid + s * k, t + s, other_ep).wait_recv()

        mine[rows:, :] = jnp.zeros((META, width), jnp.bfloat16)
        swap.wait_recv()
        mine[rows:, :LANES] = jnp.concatenate([match_in[...], hidden], axis=0).astype(jnp.bfloat16)
        for k, copy in direct:
            if k in (2, -2):
                pl.when(there(k))(copy.start)
            else:
                copy.start()

        loads[0].wait()
        loads[1].wait()
        own = mine[:rows, :]
        own_cos = table[mid, :, :LANES]
        own_sin = table[mid, :, LANES:]
        for pair in range(0, chunks, 2):
            wide = pl.ds(pair * LANES, 2 * LANES)
            product = jnp.dot(own, wq[:, wide], preferred_element_type=jnp.float32)
            for c in range(2):
                queries[:, pl.ds((pair + c) * LANES, LANES)] = turned(
                    product[:, c * LANES : (c + 1) * LANES], own_cos, own_sin
                ).astype(jnp.bfloat16)
        loads[2].wait()
        loads[3].wait()

        def project(k):
            slot = mid + s * k
            source = buf[slot, :rows, :]
            meta = buf[slot, rows:, :LANES].astype(jnp.float32)
            masks[slot] = meta[8:, :]
            cos_parts, sin_parts = [], []
            for g in range(tiles):
                picked = table[slot, 0:tile_rows, :]
                for j in range(1, tiles):
                    hit = jnp.broadcast_to(
                        jnp.concatenate([meta[j : j + 1, :]] * 2, axis=1) == g,
                        (tile_rows, 2 * LANES),
                    )
                    picked = jnp.where(
                        hit, table[slot, j * tile_rows : (j + 1) * tile_rows, :], picked
                    )
                cos_parts.append(picked[:, :LANES])
                sin_parts.append(picked[:, LANES:])
            cosine = jnp.concatenate(cos_parts, axis=0)
            sine = jnp.concatenate(sin_parts, axis=0)
            for pair in range(0, chunks, 2):
                wide = pl.ds(pair * LANES, 2 * LANES)
                product = jnp.dot(source, wk[:, wide], preferred_element_type=jnp.float32)
                for c in range(2):
                    keys[slot, :, pl.ds((pair + c) * LANES, LANES)] = turned(
                        product[:, c * LANES : (c + 1) * LANES], cosine, sine
                    ).astype(jnp.bfloat16)
                values[slot, :, wide] = jnp.dot(
                    source, wv[:, wide], preferred_element_type=jnp.float32
                ).astype(jnp.bfloat16)

        arrived(0)
        project(0)
        arrived(1)
        pl.when(there(-2))(relay_far.start)

        @pl.when(there(2))
        def _():
            arrived(2)
            relay_side.start()

        project(1)

        @pl.when(there(-2))
        def _():
            arrived(-2)

        @pl.when(there(2))
        def _():
            project(2)

        @pl.when(there(-1))
        def _():
            arrived(-1)

        pl.when(last_there)(relay_last.start)

        @pl.when(there(-2))
        def _():
            project(-2)

        @pl.when(there(-1))
        def _():
            project(-1)

        for k in (3, -3):
            @pl.when(there(k))
            def _():
                arrived(k)
                project(k)

        picks = [
            jnp.clip(stops_ref[0, 0, i] - t + BAND, 0, slots - 1) for i in range(stops_ref.shape[2])
        ]
        mask = jnp.concatenate([masks[p][0:1, :] for p in picks], axis=1)
        lane_of = lax.broadcasted_iota(jnp.int32, (rows, LANES), 1)
        for c in range(chunks):
            span = pl.ds(c * LANES, LANES)
            ask = queries[:, span]
            nothing = jnp.zeros_like(ask)
            asked = jnp.concatenate(
                [
                    jnp.where(lane_of // head_dim == h, ask, nothing)
                    for h in range(per_chunk)
                ],
                axis=0,
            )
            key_use = jnp.concatenate([keys[p, :, span] for p in picks], axis=0)
            value_use = jnp.concatenate([values[p, :, span] for p in picks], axis=0)
            raw = lax.dot_general(
                asked, key_use, (((1,), (1,)), ((), ())), preferred_element_type=jnp.float32
            )
            weights, totals = [], []
            for h in range(per_chunk):
                factor = scale_ref[c * per_chunk + h] * jnp.float32(LOG2E / math.sqrt(head_dim))
                scores = raw[h * rows : (h + 1) * rows] * factor + mask
                best = jnp.max(scores, axis=1, keepdims=True)
                weight = jnp.exp2(scores - best)
                totals.append(jnp.sum(weight, axis=1, keepdims=True))
                weights.append(weight.astype(jnp.bfloat16))
            summed = jnp.dot(
                jnp.concatenate(weights, axis=0), value_use, preferred_element_type=jnp.float32
            )
            result = summed[:rows] / totals[0]
            for h in range(1, per_chunk):
                result = jnp.where(
                    lane_of // head_dim == h, summed[h * rows : (h + 1) * rows] / totals[h], result
                )
            attended[:, span] = result.astype(jnp.bfloat16)

        loads[4].wait()
        for pair in range(0, chunks, 2):
            wide = pl.ds(pair * LANES, 2 * LANES)
            mixed = jnp.dot(attended[...], wo[:, wide], preferred_element_type=jnp.float32)
            out_ref[0, :, wide] = (
                tok_ref[0, :, wide].astype(jnp.float32) + mixed
            ).astype(jnp.bfloat16)

        swap.wait_send()
        for k, copy in direct:
            if k in (2, -2):
                pl.when(there(k))(copy.wait_send)
            else:
                copy.wait_send()
        pl.when(there(-2))(relay_far.wait_send)
        pl.when(there(2))(relay_side.wait_send)
        pl.when(last_there)(relay_last.wait_send)

    return kernel


def solution(mesh):
    blocks = mesh.shape["tok"]

    def on_device(
        tokens, norm_gain, query_weight, w_key, w_value, w_out, head_scale, matching, valid, stops
    ):
        _, rows, width = tokens.shape
        heads = head_scale.shape[0]
        tiles = matching.shape[1]
        slots = 2 * BAND + 1
        table = jnp.asarray(rotary_table(blocks, rows, width // heads))
        vmem = pl.BlockSpec(memory_space=pltpu.VMEM)
        smem = pl.BlockSpec(memory_space=pltpu.SMEM)
        anywhere = pl.BlockSpec(memory_space=pl.ANY)
        square = pltpu.VMEM((width, width), jnp.bfloat16)
        block = pltpu.VMEM((rows, width), jnp.bfloat16)
        band = pltpu.VMEM((slots, rows, width), jnp.bfloat16)
        return pl.pallas_call(
            make_kernel(blocks, rows, width, heads, tiles),
            out_shape=jax.ShapeDtypeStruct(tokens.shape, jnp.bfloat16),
            in_specs=[vmem, vmem, smem, smem, smem, smem] + [anywhere] * 5,
            out_specs=vmem,
            scratch_shapes=[
                square, square, square, square,
                pltpu.VMEM((slots, rows, 2 * LANES), jnp.float32),
                pltpu.VMEM((rows + META, width), jnp.bfloat16),
                pltpu.VMEM((slots, rows + META, width), jnp.bfloat16),
                pltpu.VMEM((8, LANES), jnp.float32),
                pltpu.VMEM((8, LANES), jnp.float32),
                block, band, band,
                pltpu.VMEM((slots, 8, rows), jnp.float32),
                block,
                pltpu.SemaphoreType.DMA((5,)),
                pltpu.SemaphoreType.DMA((7,)),
                pltpu.SemaphoreType.DMA((slots,)),
                pltpu.SemaphoreType.DMA((2,)),
            ],
            compiler_params=pltpu.CompilerParams(
                collective_id=0, has_side_effects=True, vmem_limit_bytes=60 * 1024 * 1024
            ),
            cost_estimate=pl.CostEstimate(
                flops=40 * rows * width * width, bytes_accessed=8 * width * width,
                transcendentals=heads * rows * rows * 4,
            ),
        )(
            tokens, norm_gain[None, :], head_scale, matching, valid, stops,
            query_weight, w_key, w_value, w_out, table,
        )

    in_specs = (
        P("ep", ("grp", "tok"), None),
        P(), P(), P(), P(), P(), P(),
        P("ep", ("grp", "tok")),
        P("ep", ("grp", "tok")),
        P("ep", ("grp", "tok"), None),
    )
    out_specs = P("ep", ("grp", "tok"), None)
    return jax.shard_map(
        on_device, mesh=mesh, in_specs=in_specs, out_specs=out_specs, check_vma=False
    )
```

```python
import math

import jax
import jax.numpy as jnp
import numpy as np
from jax import lax
from jax.experimental import pallas as pl
from jax.experimental.pallas import tpu as pltpu
from jax.sharding import PartitionSpec as P

BAND = 3
ROW_PATCHES = 1024
LANES = 128
META = 16
MESH = pl.DeviceIdType.MESH
LOG2E = 1.4426950408889634


def rotary_table(blocks, rows, head_dim):
    quarter = head_dim // 4
    spots = np.arange(-BAND * rows, (blocks + BAND) * rows, dtype=np.int32)
    freqs = np.float32(100.0) ** (-np.arange(quarter, dtype=np.float32) / np.float32(quarter))
    parts = []
    for coordinate in (spots // ROW_PATCHES, spots % ROW_PATCHES):
        angle = coordinate.astype(np.float32)[:, None] * freqs[None, :].astype(np.float32)
        parts.append((np.cos(angle), np.sin(angle)))
    cosine = np.concatenate([half for c, _ in parts for half in (c, c)], axis=1)
    sine = np.concatenate([half for _, s in parts for half in (-s, s)], axis=1)
    copies = LANES // head_dim
    table = np.concatenate([cosine] * copies + [sine] * copies, axis=1)
    return table.reshape(blocks + 2 * BAND, rows, 2 * LANES).astype(np.float32)


def make_kernel(blocks, rows, width, heads, tiles):
    head_dim = width // heads
    quarter = head_dim // 4
    tile_rows = rows // tiles
    chunks = width // LANES
    per_chunk = LANES // head_dim
    slots = 2 * BAND + 1

    def turned(values, cosine, sine):
        lane = lax.broadcasted_iota(jnp.int32, values.shape, 1)
        ahead = pltpu.roll(values, LANES - quarter, 1)
        behind = pltpu.roll(values, quarter, 1)
        other = jnp.where(lane % (2 * quarter) < quarter, ahead, behind)
        return values * cosine + other * sine

    def kernel(
        tok_ref, gain_ref, scale_ref, match_ref, valid_ref, stops_ref,
        wq_hbm, wk_hbm, wv_hbm, wo_hbm, table_hbm,
        out_ref,
        wq, wk, wv, wo, table, mine, buf, match_out, match_in,
        queries, keys, values, masks, attended, best_ref, total_ref, accum,
        local_sem, send_sem, recv_sem, match_sem,
    ):
        t = lax.axis_index("tok")
        ep = lax.axis_index("ep")
        other_ep = 1 - ep
        s = 1 - 2 * (t % 2)

        def there(k):
            spot = t + s * k
            return (spot >= 0) & (spot < blocks)

        def count(k):
            return there(k).astype(jnp.int32)

        loads = [
            pltpu.make_async_copy(table_hbm.at[pl.ds(t, slots)], table, local_sem.at[0]),
            pltpu.make_async_copy(wq_hbm, wq, local_sem.at[1]),
            pltpu.make_async_copy(wk_hbm, wk, local_sem.at[2]),
            pltpu.make_async_copy(wv_hbm, wv, local_sem.at[3]),
            pltpu.make_async_copy(wo_hbm, wo, local_sem.at[4]),
        ]

        barrier = pltpu.get_barrier_semaphore()

        def greet(tok, e):
            pl.semaphore_signal(
                barrier, inc=1, device_id={"tok": tok, "ep": e}, device_id_type=MESH
            )

        greet(t, other_ep)
        greet(t + s, ep)
        greet(t + s, other_ep)
        for k in (2, -2):
            @pl.when(there(k))
            def _():
                greet(t + s * k, ep)
                greet(t + s * k, other_ep)

        for load in loads:
            load.start()

        floated = tok_ref[0].astype(jnp.float32)
        center = jnp.mean(floated, axis=-1, keepdims=True)
        apart = floated - center
        spread = jnp.mean(apart * apart, axis=-1, keepdims=True)
        mine[:rows, :] = (apart * lax.rsqrt(spread + 1e-05) * gain_ref[...].reshape(1, width)).astype(jnp.bfloat16)

        row = lax.broadcasted_iota(jnp.int32, (8, LANES), 0)
        matched = jnp.zeros((8, LANES), jnp.float32)
        lane = lax.broadcasted_iota(jnp.int32, (8, rows), 1)
        live = jnp.zeros((8, rows), jnp.int32)
        for j in range(tiles):
            matched = jnp.where(row == j, match_ref[0, j].astype(jnp.float32), matched)
            live = jnp.where(lane // tile_rows == j, valid_ref[0, j], live)
        match_out[...] = matched
        hidden = jnp.where(lane % tile_rows < live, jnp.float32(0), jnp.float32(-1e30))

        pl.semaphore_wait(barrier, 3 + 2 * count(2) + 2 * count(-2))

        swap = pltpu.make_async_remote_copy(
            match_out, match_in, match_sem.at[0], match_sem.at[1],
            device_id={"tok": t, "ep": other_ep}, device_id_type=MESH,
        )
        swap.start()

        cuts = (pl.ds(0, rows // 2), pl.ds(rows // 2, rows // 2 + META))

        def piece(src, number, slot, tok, e, half):
            cut = cuts[half]
            return pltpu.make_async_remote_copy(
                src.at[cut], buf.at[slot, cut],
                send_sem.at[number, half], recv_sem.at[slot, half],
                device_id={"tok": tok, "ep": e}, device_id_type=MESH,
            )

        def transfer(src, number, slot, tok, e):
            return [piece(src, number, slot, tok, e, half) for half in range(len(cuts))]

        mid = BAND
        direct = [
            (2, transfer(mine, 0, mid - 2 * s, t + 2 * s, other_ep)),
            (-2, transfer(mine, 1, mid + 2 * s, t - 2 * s, other_ep)),
            (1, transfer(mine, 2, mid - s, t + s, other_ep)),
            (0, transfer(mine, 3, mid, t, other_ep)),
        ]
        relay_far = transfer(buf.at[mid + s], 4, mid + 3 * s, t - 2 * s, ep)
        relay_side = transfer(buf.at[mid + 2 * s], 5, mid + s, t + s, ep)
        relay_last = transfer(buf.at[mid - s], 6, mid - 3 * s, t + 2 * s, ep)
        last_there = there(2) & there(-1)

        def arrived(k, half):
            piece(mine, 0, mid + s * k, t + s, other_ep, half).wait_recv()

        def both(k):
            arrived(k, 0)
            arrived(k, 1)

        mine[rows:, :] = jnp.zeros((META, width), jnp.bfloat16)
        swap.wait_recv()
        mine[rows:, :LANES] = jnp.concatenate([match_in[...], hidden], axis=0).astype(jnp.bfloat16)
        for half in range(2):
            for k, copy in direct:
                if k in (2, -2):
                    pl.when(there(k))(copy[half].start)
                else:
                    copy[half].start()

        loads[0].wait()
        loads[1].wait()
        own = mine[:rows, :]
        own_cos = table[mid, :, :LANES]
        own_sin = table[mid, :, LANES:]
        for pair in range(0, chunks, 2):
            wide = pl.ds(pair * LANES, 2 * LANES)
            product = jnp.dot(own, wq[:, wide], preferred_element_type=jnp.float32)
            for c in range(2):
                queries[:, pl.ds((pair + c) * LANES, LANES)] = turned(
                    product[:, c * LANES : (c + 1) * LANES], own_cos, own_sin
                ).astype(jnp.bfloat16)
        loads[2].wait()
        loads[3].wait()

        def project(k):
            slot = mid + s * k
            source = buf[slot, :rows, :]
            meta = buf[slot, rows:, :LANES].astype(jnp.float32)
            masks[slot] = meta[8:, :]
            cos_parts, sin_parts = [], []
            for g in range(tiles):
                picked = table[slot, 0:tile_rows, :]
                for j in range(1, tiles):
                    hit = jnp.broadcast_to(
                        jnp.concatenate([meta[j : j + 1, :]] * 2, axis=1) == g,
                        (tile_rows, 2 * LANES),
                    )
                    picked = jnp.where(
                        hit, table[slot, j * tile_rows : (j + 1) * tile_rows, :], picked
                    )
                cos_parts.append(picked[:, :LANES])
                sin_parts.append(picked[:, LANES:])
            cosine = jnp.concatenate(cos_parts, axis=0)
            sine = jnp.concatenate(sin_parts, axis=0)
            for pair in range(0, chunks, 2):
                wide = pl.ds(pair * LANES, 2 * LANES)
                product = jnp.dot(source, wk[:, wide], preferred_element_type=jnp.float32)
                for c in range(2):
                    keys[slot, :, pl.ds((pair + c) * LANES, LANES)] = turned(
                        product[:, c * LANES : (c + 1) * LANES], cosine, sine
                    ).astype(jnp.bfloat16)
                values[slot, :, wide] = jnp.dot(
                    source, wv[:, wide], preferred_element_type=jnp.float32
                ).astype(jnp.bfloat16)

        def pass_on(half):
            arrived(1, half)
            pl.when(there(-2))(relay_far[half].start)

            @pl.when(there(2))
            def _():
                arrived(2, half)
                relay_side[half].start()

        def pass_last(half):
            @pl.when(there(-1))
            def _():
                arrived(-1, half)

            pl.when(last_there)(relay_last[half].start)

        pass_on(0)
        both(0)
        project(0)
        pass_on(1)
        project(1)

        @pl.when(there(2))
        def _():
            project(2)

        pass_last(0)

        @pl.when(there(-2))
        def _():
            both(-2)
            project(-2)

        pass_last(1)

        @pl.when(there(-1))
        def _():
            project(-1)

        ranks = []
        for i in range(stops_ref.shape[2]):
            away = jnp.clip(stops_ref[0, 0, i] - t, -BAND, BAND)
            ranks.append(2 * jnp.abs(away) + (away > 0).astype(jnp.int32))
        for low, high in ((0, 1), (2, 3), (0, 2), (1, 3), (1, 2)):
            ranks[low], ranks[high] = (
                jnp.minimum(ranks[low], ranks[high]), jnp.maximum(ranks[low], ranks[high])
            )
        order = [BAND + jnp.where(r % 2 == 1, r // 2, -(r // 2)) for r in ranks]
        lane_of = lax.broadcasted_iota(jnp.int32, (rows, LANES), 1)

        def attend(picks, first):
            mask = jnp.concatenate([masks[p][0:1, :] for p in picks], axis=1)
            for c in range(chunks):
                span = pl.ds(c * LANES, LANES)
                ask = queries[:, span]
                nothing = jnp.zeros_like(ask)
                asked = jnp.concatenate(
                    [jnp.where(lane_of // head_dim == h, ask, nothing) for h in range(per_chunk)],
                    axis=0,
                )
                key_use = jnp.concatenate([keys[p, :, span] for p in picks], axis=0)
                value_use = jnp.concatenate([values[p, :, span] for p in picks], axis=0)
                raw = lax.dot_general(
                    asked, key_use, (((1,), (1,)), ((), ())), preferred_element_type=jnp.float32
                )
                weights, totals, decays = [], [], []
                for h in range(per_chunk):
                    head = c * per_chunk + h
                    factor = scale_ref[head] * jnp.float32(LOG2E / math.sqrt(head_dim))
                    scores = raw[h * rows : (h + 1) * rows] * factor + mask
                    best = jnp.max(scores, axis=1, keepdims=True)
                    if not first:
                        before = best_ref[head, :, :1]
                        best = jnp.maximum(best, before)
                        decays.append(jnp.exp2(before - best))
                    weight = jnp.exp2(scores - best)
                    total = jnp.sum(weight, axis=1, keepdims=True)
                    if first:
                        best_ref[head] = jnp.broadcast_to(best, (rows, LANES))
                        total_ref[head] = jnp.broadcast_to(total, (rows, LANES))
                    else:
                        total = total + total_ref[head, :, :1] * decays[h]
                    totals.append(total)
                    weights.append(weight.astype(jnp.bfloat16))
                summed = jnp.dot(
                    jnp.concatenate(weights, axis=0), value_use, preferred_element_type=jnp.float32
                )
                parts = []
                for h in range(per_chunk):
                    part = summed[h * rows : (h + 1) * rows]
                    if not first:
                        part = (part + accum[:, span] * decays[h]) / totals[h]
                    parts.append(part)
                result = parts[0]
                for h in range(1, per_chunk):
                    result = jnp.where(lane_of // head_dim == h, parts[h], result)
                if first:
                    accum[:, span] = result
                else:
                    attended[:, span] = result.astype(jnp.bfloat16)

        attend(order[: BAND - 1], True)
        for k in (3, -3):
            @pl.when(there(k))
            def _():
                both(k)
                project(k)

        attend(order[BAND - 1 :], False)

        loads[4].wait()
        for pair in range(0, chunks, 2):
            wide = pl.ds(pair * LANES, 2 * LANES)
            mixed = jnp.dot(attended[...], wo[:, wide], preferred_element_type=jnp.float32)
            out_ref[0, :, wide] = (
                tok_ref[0, :, wide].astype(jnp.float32) + mixed
            ).astype(jnp.bfloat16)

        swap.wait_send()
        for half in range(2):
            for k, copy in direct:
                if k in (2, -2):
                    pl.when(there(k))(copy[half].wait_send)
                else:
                    copy[half].wait_send()
            pl.when(there(-2))(relay_far[half].wait_send)
            pl.when(there(2))(relay_side[half].wait_send)
            pl.when(last_there)(relay_last[half].wait_send)

    return kernel


def solution(mesh):
    blocks = mesh.shape["tok"]

    def on_device(
        tokens, norm_gain, query_weight, w_key, w_value, w_out, head_scale, matching, valid, stops
    ):
        _, rows, width = tokens.shape
        heads = head_scale.shape[0]
        tiles = matching.shape[1]
        slots = 2 * BAND + 1
        table = jnp.asarray(rotary_table(blocks, rows, width // heads))
        vmem = pl.BlockSpec(memory_space=pltpu.VMEM)
        smem = pl.BlockSpec(memory_space=pltpu.SMEM)
        anywhere = pl.BlockSpec(memory_space=pl.ANY)
        square = pltpu.VMEM((width, width), jnp.bfloat16)
        block = pltpu.VMEM((rows, width), jnp.bfloat16)
        band = pltpu.VMEM((slots, rows, width), jnp.bfloat16)
        return pl.pallas_call(
            make_kernel(blocks, rows, width, heads, tiles),
            out_shape=jax.ShapeDtypeStruct(tokens.shape, jnp.bfloat16),
            in_specs=[vmem, vmem, smem, smem, smem, smem] + [anywhere] * 5,
            out_specs=vmem,
            scratch_shapes=[
                square, square, square, square,
                pltpu.VMEM((slots, rows, 2 * LANES), jnp.float32),
                pltpu.VMEM((rows + META, width), jnp.bfloat16),
                pltpu.VMEM((slots, rows + META, width), jnp.bfloat16),
                pltpu.VMEM((8, LANES), jnp.float32),
                pltpu.VMEM((8, LANES), jnp.float32),
                block, band, band,
                pltpu.VMEM((slots, 8, rows), jnp.float32),
                block,
                pltpu.VMEM((heads, rows, LANES), jnp.float32),
                pltpu.VMEM((heads, rows, LANES), jnp.float32),
                pltpu.VMEM((rows, width), jnp.float32),
                pltpu.SemaphoreType.DMA((5,)),
                pltpu.SemaphoreType.DMA((7, 2)),
                pltpu.SemaphoreType.DMA((slots, 2)),
                pltpu.SemaphoreType.DMA((2,)),
            ],
            compiler_params=pltpu.CompilerParams(
                collective_id=0, has_side_effects=True, vmem_limit_bytes=60 * 1024 * 1024
            ),
            cost_estimate=pl.CostEstimate(
                flops=40 * rows * width * width, bytes_accessed=8 * width * width,
                transcendentals=heads * rows * rows * 4,
            ),
        )(
            tokens, norm_gain, head_scale, matching, valid, stops,
            query_weight, w_key, w_value, w_out, table,
        )

    in_specs = (
        P("ep", ("grp", "tok"), None),
        P(), P(), P(), P(), P(), P(),
        P("ep", ("grp", "tok")),
        P("ep", ("grp", "tok")),
        P("ep", ("grp", "tok"), None),
    )
    out_specs = P("ep", ("grp", "tok"), None)
    return jax.shard_map(
        on_device, mesh=mesh, in_specs=in_specs, out_specs=out_specs, check_vma=False
    )
```

```python
import math

import jax
import jax.numpy as jnp
import numpy as np
from jax import lax
from jax.experimental import pallas as pl
from jax.experimental.pallas import tpu as pltpu
from jax.sharding import PartitionSpec as P

BAND = 3
ROW_PATCHES = 1024
LANES = 128
META = 16
MESH = pl.DeviceIdType.MESH
LOG2E = 1.4426950408889634


def rotary_table(blocks, rows, head_dim):
    quarter = head_dim // 4
    spots = np.arange(-BAND * rows, (blocks + BAND) * rows, dtype=np.int32)
    freqs = np.float32(100.0) ** (-np.arange(quarter, dtype=np.float32) / np.float32(quarter))
    parts = []
    for coordinate in (spots // ROW_PATCHES, spots % ROW_PATCHES):
        angle = coordinate.astype(np.float32)[:, None] * freqs[None, :].astype(np.float32)
        parts.append((np.cos(angle), np.sin(angle)))
    cosine = np.concatenate([half for c, _ in parts for half in (c, c)], axis=1)
    sine = np.concatenate([half for _, s in parts for half in (-s, s)], axis=1)
    copies = LANES // head_dim
    table = np.concatenate([cosine] * copies + [sine] * copies, axis=1)
    return table.reshape(blocks + 2 * BAND, rows, 2 * LANES).astype(np.float32)


def make_kernel(blocks, rows, width, heads, tiles):
    head_dim = width // heads
    quarter = head_dim // 4
    tile_rows = rows // tiles
    chunks = width // LANES
    per_chunk = LANES // head_dim
    slots = 2 * BAND + 1

    def turned(values, cosine, sine):
        lane = lax.broadcasted_iota(jnp.int32, values.shape, 1)
        ahead = pltpu.roll(values, LANES - quarter, 1)
        behind = pltpu.roll(values, quarter, 1)
        other = jnp.where(lane % (2 * quarter) < quarter, ahead, behind)
        return values * cosine + other * sine

    def kernel(
        tok_ref, gain_ref, scale_ref, match_ref, valid_ref, stops_ref,
        wq_hbm, wk_hbm, wv_hbm, wo_hbm, table_hbm,
        out_ref,
        wq, wk, wv, wo, table, mine, buf, match_out, match_in,
        queries, keys, values, masks, attended, best_ref, total_ref, accum,
        local_sem, send_sem, recv_sem, match_sem,
    ):
        t = lax.axis_index("tok")
        ep = lax.axis_index("ep")
        other_ep = 1 - ep
        s = 1 - 2 * (t % 2)

        def there(k):
            spot = t + s * k
            return (spot >= 0) & (spot < blocks)

        def count(k):
            return there(k).astype(jnp.int32)

        loads = [
            pltpu.make_async_copy(table_hbm.at[pl.ds(t, slots)], table, local_sem.at[0]),
            pltpu.make_async_copy(wq_hbm, wq, local_sem.at[1]),
            pltpu.make_async_copy(wk_hbm, wk, local_sem.at[2]),
            pltpu.make_async_copy(wv_hbm, wv, local_sem.at[3]),
            pltpu.make_async_copy(wo_hbm, wo, local_sem.at[4]),
        ]

        barrier = pltpu.get_barrier_semaphore()

        def greet(tok, e):
            pl.semaphore_signal(
                barrier, inc=1, device_id={"tok": tok, "ep": e}, device_id_type=MESH
            )

        greet(t, other_ep)
        greet(t + s, ep)
        greet(t + s, other_ep)
        for k in (2, -2):
            @pl.when(there(k))
            def _():
                greet(t + s * k, ep)
                greet(t + s * k, other_ep)

        for load in loads:
            load.start()

        floated = tok_ref[0].astype(jnp.float32)
        center = jnp.mean(floated, axis=-1, keepdims=True)
        apart = floated - center
        spread = jnp.mean(apart * apart, axis=-1, keepdims=True)
        mine[:rows, :] = (apart * lax.rsqrt(spread + 1e-05) * gain_ref[...].reshape(1, width)).astype(jnp.bfloat16)

        row = lax.broadcasted_iota(jnp.int32, (8, LANES), 0)
        matched = jnp.zeros((8, LANES), jnp.float32)
        lane = lax.broadcasted_iota(jnp.int32, (8, rows), 1)
        live = jnp.zeros((8, rows), jnp.int32)
        for j in range(tiles):
            matched = jnp.where(row == j, match_ref[0, j].astype(jnp.float32), matched)
            live = jnp.where(lane // tile_rows == j, valid_ref[0, j], live)
        match_out[...] = matched
        hidden = jnp.where(lane % tile_rows < live, jnp.float32(0), jnp.float32(-1e30))

        pl.semaphore_wait(barrier, 3 + 2 * count(2) + 2 * count(-2))

        swap = pltpu.make_async_remote_copy(
            match_out, match_in, match_sem.at[0], match_sem.at[1],
            device_id={"tok": t, "ep": other_ep}, device_id_type=MESH,
        )
        swap.start()

        cuts = (pl.ds(0, rows // 2), pl.ds(rows // 2, rows // 2 + META))

        def piece(src, number, slot, tok, e, half):
            cut = cuts[half]
            return pltpu.make_async_remote_copy(
                src.at[cut], buf.at[slot, cut],
                send_sem.at[number, half], recv_sem.at[slot, half],
                device_id={"tok": tok, "ep": e}, device_id_type=MESH,
            )

        def transfer(src, number, slot, tok, e):
            return [piece(src, number, slot, tok, e, half) for half in range(len(cuts))]

        mid = BAND
        direct = [
            (2, transfer(mine, 0, mid - 2 * s, t + 2 * s, other_ep)),
            (-2, transfer(mine, 1, mid + 2 * s, t - 2 * s, other_ep)),
            (1, transfer(mine, 2, mid - s, t + s, other_ep)),
            (0, transfer(mine, 3, mid, t, other_ep)),
        ]
        relay_far = transfer(buf.at[mid + s], 4, mid + 3 * s, t - 2 * s, ep)
        relay_side = transfer(buf.at[mid + 2 * s], 5, mid + s, t + s, ep)
        relay_last = transfer(buf.at[mid - s], 6, mid - 3 * s, t + 2 * s, ep)
        last_there = there(2) & there(-1)

        def arrived(k, half):
            piece(mine, 0, mid + s * k, t + s, other_ep, half).wait_recv()

        def both(k):
            arrived(k, 0)
            arrived(k, 1)

        def send(half):
            for k, copy in direct:
                if k in (2, -2):
                    pl.when(there(k))(copy[half].start)
                else:
                    copy[half].start()

        send(0)
        mine[rows:, :] = jnp.zeros((META, width), jnp.bfloat16)
        swap.wait_recv()
        mine[rows:, :LANES] = jnp.concatenate([match_in[...], hidden], axis=0).astype(jnp.bfloat16)
        send(1)

        loads[0].wait()
        loads[1].wait()
        own = mine[:rows, :]
        own_cos = table[mid, :, :LANES]
        own_sin = table[mid, :, LANES:]
        for pair in range(0, chunks, 2):
            wide = pl.ds(pair * LANES, 2 * LANES)
            product = jnp.dot(own, wq[:, wide], preferred_element_type=jnp.float32)
            for c in range(2):
                queries[:, pl.ds((pair + c) * LANES, LANES)] = turned(
                    product[:, c * LANES : (c + 1) * LANES], own_cos, own_sin
                ).astype(jnp.bfloat16)
        loads[2].wait()
        loads[3].wait()

        def project(k):
            slot = mid + s * k
            source = buf[slot, :rows, :]
            meta = buf[slot, rows:, :LANES].astype(jnp.float32)
            masks[slot] = meta[8:, :]
            cos_parts, sin_parts = [], []
            for g in range(tiles):
                picked = table[slot, 0:tile_rows, :]
                for j in range(1, tiles):
                    hit = jnp.broadcast_to(
                        jnp.concatenate([meta[j : j + 1, :]] * 2, axis=1) == g,
                        (tile_rows, 2 * LANES),
                    )
                    picked = jnp.where(
                        hit, table[slot, j * tile_rows : (j + 1) * tile_rows, :], picked
                    )
                cos_parts.append(picked[:, :LANES])
                sin_parts.append(picked[:, LANES:])
            cosine = jnp.concatenate(cos_parts, axis=0)
            sine = jnp.concatenate(sin_parts, axis=0)
            for pair in range(0, chunks, 2):
                wide = pl.ds(pair * LANES, 2 * LANES)
                product = jnp.dot(source, wk[:, wide], preferred_element_type=jnp.float32)
                for c in range(2):
                    keys[slot, :, pl.ds((pair + c) * LANES, LANES)] = turned(
                        product[:, c * LANES : (c + 1) * LANES], cosine, sine
                    ).astype(jnp.bfloat16)
                values[slot, :, wide] = jnp.dot(
                    source, wv[:, wide], preferred_element_type=jnp.float32
                ).astype(jnp.bfloat16)

        def pass_on(half):
            arrived(1, half)
            pl.when(there(-2))(relay_far[half].start)

            @pl.when(there(2))
            def _():
                arrived(2, half)
                relay_side[half].start()

        def pass_last(half):
            @pl.when(there(-1))
            def _():
                arrived(-1, half)

            pl.when(last_there)(relay_last[half].start)

        pass_on(0)
        both(0)
        project(0)
        pass_on(1)
        project(1)

        @pl.when(there(2))
        def _():
            project(2)

        pass_last(0)

        @pl.when(there(-2))
        def _():
            both(-2)
            project(-2)

        pass_last(1)

        @pl.when(there(-1))
        def _():
            project(-1)

        ranks = []
        for i in range(stops_ref.shape[2]):
            away = jnp.clip(stops_ref[0, 0, i] - t, -BAND, BAND)
            ranks.append(2 * jnp.abs(away) + (away > 0).astype(jnp.int32))
        for low, high in ((0, 1), (2, 3), (0, 2), (1, 3), (1, 2)):
            ranks[low], ranks[high] = (
                jnp.minimum(ranks[low], ranks[high]), jnp.maximum(ranks[low], ranks[high])
            )
        order = [BAND + jnp.where(r % 2 == 1, r // 2, -(r // 2)) for r in ranks]
        lane_of = lax.broadcasted_iota(jnp.int32, (rows, LANES), 1)

        def attend(picks, first):
            mask = jnp.concatenate([masks[p][0:1, :] for p in picks], axis=1)
            for c in range(chunks):
                span = pl.ds(c * LANES, LANES)
                ask = queries[:, span]
                nothing = jnp.zeros_like(ask)
                asked = jnp.concatenate(
                    [jnp.where(lane_of // head_dim == h, ask, nothing) for h in range(per_chunk)],
                    axis=0,
                )
                key_use = jnp.concatenate([keys[p, :, span] for p in picks], axis=0)
                value_use = jnp.concatenate([values[p, :, span] for p in picks], axis=0)
                raw = lax.dot_general(
                    asked, key_use, (((1,), (1,)), ((), ())), preferred_element_type=jnp.float32
                )
                weights, totals, decays = [], [], []
                for h in range(per_chunk):
                    head = c * per_chunk + h
                    factor = scale_ref[head] * jnp.float32(LOG2E / math.sqrt(head_dim))
                    scores = raw[h * rows : (h + 1) * rows] * factor + mask
                    best = jnp.max(scores, axis=1, keepdims=True)
                    if not first:
                        before = best_ref[head, :, :1]
                        best = jnp.maximum(best, before)
                        decays.append(jnp.exp2(before - best))
                    weight = jnp.exp2(scores - best)
                    total = jnp.sum(weight, axis=1, keepdims=True)
                    if first:
                        best_ref[head] = jnp.broadcast_to(best, (rows, LANES))
                        total_ref[head] = jnp.broadcast_to(total, (rows, LANES))
                    else:
                        total = total + total_ref[head, :, :1] * decays[h]
                    totals.append(total)
                    weights.append(weight.astype(jnp.bfloat16))
                summed = jnp.dot(
                    jnp.concatenate(weights, axis=0), value_use, preferred_element_type=jnp.float32
                )
                parts = []
                for h in range(per_chunk):
                    part = summed[h * rows : (h + 1) * rows]
                    if not first:
                        part = (part + accum[:, span] * decays[h]) / totals[h]
                    parts.append(part)
                result = parts[0]
                for h in range(1, per_chunk):
                    result = jnp.where(lane_of // head_dim == h, parts[h], result)
                if first:
                    accum[:, span] = result
                else:
                    attended[:, span] = result.astype(jnp.bfloat16)

        attend(order[: BAND - 1], True)
        for k in (3, -3):
            @pl.when(there(k))
            def _():
                both(k)
                project(k)

        attend(order[BAND - 1 :], False)

        loads[4].wait()
        for pair in range(0, chunks, 2):
            wide = pl.ds(pair * LANES, 2 * LANES)
            mixed = jnp.dot(attended[...], wo[:, wide], preferred_element_type=jnp.float32)
            out_ref[0, :, wide] = (
                tok_ref[0, :, wide].astype(jnp.float32) + mixed
            ).astype(jnp.bfloat16)

        swap.wait_send()
        for half in range(2):
            for k, copy in direct:
                if k in (2, -2):
                    pl.when(there(k))(copy[half].wait_send)
                else:
                    copy[half].wait_send()
            pl.when(there(-2))(relay_far[half].wait_send)
            pl.when(there(2))(relay_side[half].wait_send)
            pl.when(last_there)(relay_last[half].wait_send)

    return kernel


def solution(mesh):
    blocks = mesh.shape["tok"]

    def on_device(
        tokens, norm_gain, query_weight, w_key, w_value, w_out, head_scale, matching, valid, stops
    ):
        _, rows, width = tokens.shape
        heads = head_scale.shape[0]
        tiles = matching.shape[1]
        slots = 2 * BAND + 1
        table = jnp.asarray(rotary_table(blocks, rows, width // heads))
        vmem = pl.BlockSpec(memory_space=pltpu.VMEM)
        smem = pl.BlockSpec(memory_space=pltpu.SMEM)
        anywhere = pl.BlockSpec(memory_space=pl.ANY)
        square = pltpu.VMEM((width, width), jnp.bfloat16)
        block = pltpu.VMEM((rows, width), jnp.bfloat16)
        band = pltpu.VMEM((slots, rows, width), jnp.bfloat16)
        return pl.pallas_call(
            make_kernel(blocks, rows, width, heads, tiles),
            out_shape=jax.ShapeDtypeStruct(tokens.shape, jnp.bfloat16),
            in_specs=[vmem, vmem, smem, smem, smem, smem] + [anywhere] * 5,
            out_specs=vmem,
            scratch_shapes=[
                square, square, square, square,
                pltpu.VMEM((slots, rows, 2 * LANES), jnp.float32),
                pltpu.VMEM((rows + META, width), jnp.bfloat16),
                pltpu.VMEM((slots, rows + META, width), jnp.bfloat16),
                pltpu.VMEM((8, LANES), jnp.float32),
                pltpu.VMEM((8, LANES), jnp.float32),
                block, band, band,
                pltpu.VMEM((slots, 8, rows), jnp.float32),
                block,
                pltpu.VMEM((heads, rows, LANES), jnp.float32),
                pltpu.VMEM((heads, rows, LANES), jnp.float32),
                pltpu.VMEM((rows, width), jnp.float32),
                pltpu.SemaphoreType.DMA((5,)),
                pltpu.SemaphoreType.DMA((7, 2)),
                pltpu.SemaphoreType.DMA((slots, 2)),
                pltpu.SemaphoreType.DMA((2,)),
            ],
            compiler_params=pltpu.CompilerParams(
                collective_id=0, has_side_effects=True, vmem_limit_bytes=60 * 1024 * 1024
            ),
            cost_estimate=pl.CostEstimate(
                flops=40 * rows * width * width, bytes_accessed=8 * width * width,
                transcendentals=heads * rows * rows * 4,
            ),
        )(
            tokens, norm_gain, head_scale, matching, valid, stops,
            query_weight, w_key, w_value, w_out, table,
        )

    in_specs = (
        P("ep", ("grp", "tok"), None),
        P(), P(), P(), P(), P(), P(),
        P("ep", ("grp", "tok")),
        P("ep", ("grp", "tok")),
        P("ep", ("grp", "tok"), None),
    )
    out_specs = P("ep", ("grp", "tok"), None)
    return jax.shard_map(
        on_device, mesh=mesh, in_specs=in_specs, out_specs=out_specs, check_vma=False
    )
```
